32 devices in a mesh: dp: 2 (over y), row: 2 (over x), col: 8 (over z, core).
Axes of the slice: x: 2, y: 2, z: 4, core: 2. Of those that a mesh axis runs over, the one named last changes fastest.
Arguments:
- view_a: bfloat16 [256, 32768], P('dp', ('row', 'col')), may hold values from -22 to 22
- view_b: bfloat16 [256, 32768], P('dp', ('row', 'col')), may hold values from -22 to 22
Outputs:
- grad_a: float32 [256, 32768], P('dp', ('row', 'col'))
- grad_b: float32 [256, 32768], P('dp', ('row', 'col'))
- objective: float32 [], replicated
The draws below stay inside these ranges and needn't reach their ends.
All inputs are finite; a program needn't handle non-finite values.
Results may differ from the reference program's by a relative error of at most 0.0028.
Values may be sent and summed in bfloat16 or wider, within the bound.
A program may use at most 64 MiB of HBM per device.

```python
import math
import jax
import jax.numpy as jnp
from jax import lax

F = 32768
N = 256


def shared_parts(key):
    keys = jax.random.split(jax.random.fold_in(key, 11), 4)
    pick = jax.random.randint(keys[0], (F,), 0, 2)
    low_part = jax.random.uniform(keys[1], (F,), jnp.float32, -1.6, -0.7)
    high_part = jax.random.uniform(keys[2], (F,), jnp.float32, 0.7, 1.2)
    scale = jnp.exp(jnp.where(pick == 1, high_part, low_part))
    offset = jax.random.uniform(keys[3], (F,), jnp.float32, -1.0, 1.0)
    return (scale, offset)


def rough(key):
    first = jax.random.fold_in(key, 0)
    normal_part = jax.random.truncated_normal(first, -4.0, 4.0, (N, F), jnp.float32)
    return normal_part


def build_view(key, own_key):
    scale, offset = shared_parts(key)
    common = rough(jax.random.fold_in(key, 21))
    own = rough(own_key)
    value = scale * (offset + (common + 0.5 * own) / math.sqrt(1.25))
    return value.astype(jnp.bfloat16)


def draw_view_a(key, part):
    own_key = jax.random.fold_in(key, 1)
    return build_view(key, own_key)


def draw_view_b(key, part):
    own_key = jax.random.fold_in(key, 2)
    return build_view(key, own_key)


def setup_inputs(seed: int = 0) -> dict:
    arg_keys = jax.random.split(jax.random.key(seed), 3)
    return {
        "view_a": draw_view_a(jax.random.fold_in(arg_keys[2], 71), 0),
        "view_b": draw_view_b(jax.random.fold_in(arg_keys[2], 71), 0),
    }


def view_terms(z):
    zf = z.astype(jnp.float32)
    mean = lax.optimization_barrier(jnp.mean(zf, axis=0))
    diff = zf - mean
    std = jnp.sqrt(lax.optimization_barrier(jnp.sum(diff * diff, axis=0)) / (N - 1) + 0.0001)
    centered = diff.astype(jnp.bfloat16)
    block = min(1024, F)
    col_ids = jnp.arange(F, dtype=jnp.int32)

    def step(carry, index):
        pull, square = carry
        start = (index * block).astype(jnp.int32)
        rows = lax.dynamic_slice_in_dim(centered, start, block, 1)
        cov = lax.dot_general(rows, centered, (((0,), (0,)), ((), ())), preferred_element_type=jnp.float32) / (N - 1)
        row_ids = start + jnp.arange(block, dtype=jnp.int32)
        off = jnp.where(row_ids[:, None] == col_ids[None, :], jnp.float32(0.0), cov)
        square = square + jnp.sum(off * off)
        pull = pull + jnp.dot(rows.astype(jnp.float32), off, preferred_element_type=jnp.float32, precision=lax.Precision.HIGHEST)
        return ((pull, square), None)
    init = (jnp.zeros((N, F), jnp.float32), jnp.zeros((), jnp.float32))
    (pull, square), unused = lax.scan(step, init, jnp.arange(F // block, dtype=jnp.int32))
    return (diff, std, pull, square)

def reference(view_a, view_b):
    diff_a, std_a, pull_a, square_a = view_terms(view_a)
    diff_b, std_b, pull_b, square_b = view_terms(view_b)
    gap = view_a.astype(jnp.float32) - view_b.astype(jnp.float32)
    coef = 2.0 * N / (25.0 * (N - 1))
    hinge_a = jnp.where(std_a < 1.0, N * diff_a / (2.0 * std_a * (N - 1)), jnp.float32(0.0))
    hinge_b = jnp.where(std_b < 1.0, N * diff_b / (2.0 * std_b * (N - 1)), jnp.float32(0.0))
    grad_a = gap - hinge_a + coef * (pull_a - lax.optimization_barrier(jnp.mean(pull_a, axis=0)))
    grad_b = -gap - hinge_b + coef * (pull_b - lax.optimization_barrier(jnp.mean(pull_b, axis=0)))
    loss = 25.0 * jnp.sum(gap * gap) / (N * F)
    loss = loss + 25.0 * (jnp.sum(jnp.maximum(1.0 - std_a, 0.0)) + jnp.sum(jnp.maximum(1.0 - std_b, 0.0))) / F
    loss = loss + (square_a + square_b) / F
    objective = loss * N / (50.0 * F)
    return (grad_a, grad_b, objective)
```

```python
import jax
import jax.numpy as jnp
from jax import lax
from jax.sharding import PartitionSpec as P


def on_device(view_a, view_b):
    n_dp = lax.axis_size("dp")
    n_parts = lax.axis_size("row") * lax.axis_size("col")
    dp_index = lax.axis_index("dp")
    n_dev, shard = view_a.shape
    total = n_dev * n_dp
    f_all = shard * n_parts
    coef = 2.0 * total / (25.0 * (total - 1))
    share = shard // n_dp

    own = jnp.stack([view_a, view_b])
    full = lax.all_gather(own, "dp", axis=1, tiled=True).astype(jnp.float32)
    mean = jnp.sum(full, axis=1, keepdims=True) / total
    diff = full - mean
    std = jnp.sqrt(jnp.sum(diff * diff, axis=1, keepdims=True) / (total - 1) + 0.0001)
    cent = diff.astype(jnp.bfloat16)
    cent32 = cent.astype(jnp.float32)
    diag = jnp.sum(cent32 * cent32, axis=1, keepdims=True) / (total - 1)

    piece = lax.dynamic_slice_in_dim(cent, dp_index * share, share, 2)
    gram = lax.dot_general(
        piece, piece, (((2,), (2,)), ((0,), (0,))), preferred_element_type=jnp.float32
    )
    own32 = own.astype(jnp.float32)
    gap = own32[0] - own32[1]
    local = 25.0 * jnp.sum(gap * gap) / (total * f_all)
    per_feature = 25.0 * jnp.maximum(1.0 - std, 0.0) - diag * diag
    local = local + jnp.sum(per_feature) / (f_all * n_dp)
    gram, local = lax.psum((gram, local), ("dp", "row", "col"))
    gram = gram / (total - 1)
    objective = (local + jnp.sum(gram * gram) / f_all) * total / (50.0 * f_all)

    lean = gram - jnp.mean(gram, axis=1, keepdims=True)
    lean = lax.dynamic_slice_in_dim(lean, dp_index * n_dev, n_dev, 1)
    pull = lax.dot_general(
        lean,
        cent32,
        (((2,), (1,)), ((0,), (0,))),
        preferred_element_type=jnp.float32,
        precision=lax.Precision.HIGHEST,
    )
    mine = lax.dynamic_slice_in_dim(cent32, dp_index * n_dev, n_dev, 1)
    pull = pull - diag * (mine - jnp.mean(cent32, axis=1, keepdims=True))
    hinge = jnp.where(std < 1.0, total * (own32 - mean) / (2.0 * std * (total - 1)), 0.0)
    rest = coef * pull - hinge
    return (gap + rest[0], rest[1] - gap, objective)


def solution(mesh):
    in_specs = (P("dp", ("row", "col")), P("dp", ("row", "col")))
    out_specs = (P("dp", ("row", "col")), P("dp", ("row", "col")), P())
    return jax.shard_map(
        on_device, mesh=mesh, in_specs=in_specs, out_specs=out_specs, check_vma=False
    )
```

```python
import functools

import jax
import jax.numpy as jnp
from jax import lax
from jax.experimental import pallas as pl
from jax.experimental.pallas import tpu as pltpu
from jax.sharding import PartitionSpec as P

LANES = 128
TILE = 8
MESH = pl.DeviceIdType.MESH


def plain(view_a, view_b):
    n_dp = lax.axis_size("dp")
    n_parts = lax.axis_size("row") * lax.axis_size("col")
    dp_index = lax.axis_index("dp")
    n_dev, shard = view_a.shape
    total = n_dev * n_dp
    f_all = shard * n_parts
    coef = 2.0 * total / (25.0 * (total - 1))
    share = shard // n_dp

    own = jnp.stack([view_a, view_b])
    full = lax.all_gather(own, "dp", axis=1, tiled=True).astype(jnp.float32)
    mean = jnp.sum(full, axis=1, keepdims=True) / total
    diff = full - mean
    std = jnp.sqrt(jnp.sum(diff * diff, axis=1, keepdims=True) / (total - 1) + 0.0001)
    cent = diff.astype(jnp.bfloat16)
    cent32 = cent.astype(jnp.float32)
    diag = jnp.sum(cent32 * cent32, axis=1, keepdims=True) / (total - 1)

    piece = lax.dynamic_slice_in_dim(cent, dp_index * share, share, 2)
    gram = lax.dot_general(
        piece, piece, (((2,), (2,)), ((0,), (0,))), preferred_element_type=jnp.float32
    )
    own32 = own.astype(jnp.float32)
    gap = own32[0] - own32[1]
    local = 25.0 * jnp.sum(gap * gap) / (total * f_all)
    per_feature = 25.0 * jnp.maximum(1.0 - std, 0.0) - diag * diag
    local = local + jnp.sum(per_feature) / (f_all * n_dp)
    gram, local = lax.psum((gram, local), ("dp", "row", "col"))
    gram = gram / (total - 1)
    objective = (local + jnp.sum(gram * gram) / f_all) * total / (50.0 * f_all)

    lean = gram - jnp.mean(gram, axis=1, keepdims=True)
    lean = lax.dynamic_slice_in_dim(lean, dp_index * n_dev, n_dev, 1)
    pull = lax.dot_general(
        lean,
        cent32,
        (((2,), (1,)), ((0,), (0,))),
        preferred_element_type=jnp.float32,
        precision=lax.Precision.HIGHEST,
    )
    mine = lax.dynamic_slice_in_dim(cent32, dp_index * n_dev, n_dev, 1)
    pull = pull - diag * (mine - jnp.mean(cent32, axis=1, keepdims=True))
    hinge = jnp.where(std < 1.0, total * (own32 - mean) / (2.0 * std * (total - 1)), 0.0)
    rest = coef * pull - hinge
    return (gap + rest[0], rest[1] - gap, objective)


def gram_kernel(
    n_row,
    n_col,
    view_a,
    view_b,
    grad_a,
    grad_b,
    loss_out,
    other,
    cent,
    stats,
    gram,
    extra,
    local,
    outgoing,
    incoming,
    summed,
    loss_in,
    view_send,
    view_recv,
    part_send,
    part_recv,
    sum_send,
    sum_recv,
    loss_send,
    loss_recv,
):
    views = (view_a, view_b)
    n_dev, shard = view_a.shape
    total = 2 * n_dev
    n_plane = n_row * n_col
    f_all = shard * n_plane
    coef = 2.0 * total / (25.0 * (total - 1))
    n_chunks = other.shape[0]
    width = other.shape[3]
    rows = summed.shape[1]
    dp = lax.axis_index("dp")
    me = lax.axis_index("row") * n_col + lax.axis_index("col")
    partner = {"dp": 1 - dp}

    def place(peer):
        return {"row": peer // n_col, "col": peer % n_col}

    barrier = pltpu.get_barrier_semaphore()
    pl.semaphore_signal(barrier, inc=1, device_id=partner, device_id_type=MESH)

    def greet(k, carry):
        peer = (me + k) % n_plane
        pl.semaphore_signal(barrier, inc=1, device_id=place(peer), device_id_type=MESH)
        return carry

    lax.fori_loop(1, n_plane, greet, 0)
    pl.semaphore_wait(barrier, n_plane)

    def view_copy(v, c):
        return pltpu.make_async_remote_copy(
            src_ref=views[v].at[:, pl.ds(pl.multiple_of(c * width, width), width)],
            dst_ref=other.at[c, v],
            send_sem=view_send.at[c, v],
            recv_sem=view_recv.at[c, v],
            device_id=partner,
            device_id_type=MESH,
        )

    def send_views(c, carry):
        view_copy(0, c).start()
        view_copy(1, c).start()
        return carry

    lax.fori_loop(0, n_chunks, send_views, 0)
    gram[...] = jnp.zeros_like(gram)
    extra[...] = jnp.zeros_like(extra)
    local[...] = jnp.zeros_like(local)

    def over(x, y):
        return jnp.sum(x, axis=0, keepdims=True) + jnp.sum(y, axis=0, keepdims=True)

    def take_chunk(c, carry):
        cols = pl.ds(pl.multiple_of(c * width, width), width)
        values = []
        for v in range(2):
            view_copy(v, c).wait()
            mine = views[v][:, cols].astype(jnp.float32)
            theirs = other[c, v].astype(jnp.float32)
            values.append((mine, theirs))
            mean = over(mine, theirs) / total
            mine = mine - mean
            theirs = theirs - mean
            std = jnp.sqrt(over(mine * mine, theirs * theirs) / (total - 1) + 0.0001)
            cent[v, 0:n_dev, cols] = mine.astype(jnp.bfloat16)
            cent[v, n_dev:total, cols] = theirs.astype(jnp.bfloat16)
            mine = cent[v, 0:n_dev, cols].astype(jnp.float32)
            theirs = cent[v, n_dev:total, cols].astype(jnp.float32)
            diag = over(mine * mine, theirs * theirs) / (total - 1)
            column = over(mine, theirs)
            stats[v, 0:1, cols] = mean
            stats[v, 1:2, cols] = jnp.where(std < 1.0, total / (2.0 * std * (total - 1)), 0.0)
            stats[v, 2:3, cols] = diag * coef
            stats[v, 3:4, cols] = column / total
            local[...] += (25.0 * jnp.maximum(1.0 - std, 0.0) - diag * diag) / f_all
            high = column.astype(jnp.bfloat16).astype(jnp.float32)
            row = lax.broadcasted_iota(jnp.int32, (16, width), 0)
            parts = jnp.where(row == 0, high, jnp.where(row == 1, column - high, 0.0))
            both = cent[v, :, cols]
            dims = (((1,), (1,)), ((), ()))
            gram[v] += lax.dot_general(
                cent[v, 0:n_dev, cols], both, dims, preferred_element_type=jnp.float32
            )
            extra[v] += lax.dot_general(
                parts.astype(jnp.bfloat16), both, dims, preferred_element_type=jnp.float32
            )
        gap_mine = values[0][0] - values[1][0]
        gap_theirs = values[0][1] - values[1][1]
        local[...] += 25.0 * over(gap_mine * gap_mine, gap_theirs * gap_theirs) / (total * f_all)
        return carry

    lax.fori_loop(0, n_chunks, take_chunk, 0)

    small = [jnp.sum(extra[v], axis=0, keepdims=True) for v in range(2)]
    local_sum = jnp.broadcast_to(jnp.sum(local[...]).reshape(1, 1), (1, LANES))
    tail = jnp.concatenate(
        [small[v][:, h * LANES:(h + 1) * LANES] for v in range(2) for h in range(2)]
        + [local_sum, jnp.zeros((TILE - 5, LANES), jnp.float32)],
        axis=0,
    )
    per_block = n_dev // rows
    for r in range(n_plane):
        v, h, q = r // (2 * per_block), r // per_block % 2, r % per_block
        outgoing[r, 0:rows, :] = gram[v, q * rows:(q + 1) * rows, h * LANES:(h + 1) * LANES]
        outgoing[r, rows:rows + TILE, :] = tail

    def part_copy(peer, slot):
        return pltpu.make_async_remote_copy(
            src_ref=outgoing.at[peer],
            dst_ref=incoming.at[slot],
            send_sem=part_send.at[peer],
            recv_sem=part_recv.at[slot],
            device_id=place(peer),
            device_id_type=MESH,
        )

    def start_part(k, carry):
        part_copy((me + k) % n_plane, me).start()
        return carry

    def end_part(k, carry):
        peer = (me + k) % n_plane
        part_copy(peer, peer).wait()
        return carry

    lax.fori_loop(1, n_plane, start_part, 0)
    incoming[me] = outgoing[me]
    lax.fori_loop(1, n_plane, end_part, 0)
    piece = incoming[0]
    for r in range(1, n_plane):
        piece = piece + incoming[r]
    summed[me] = piece[0:rows, :]
    tail = piece[rows:rows + TILE, :]

    def sum_copy(peer, slot):
        return pltpu.make_async_remote_copy(
            src_ref=summed.at[slot],
            dst_ref=summed.at[slot],
            send_sem=sum_send.at[peer],
            recv_sem=sum_recv.at[slot],
            device_id=place(peer),
            device_id_type=MESH,
        )

    def start_sum(k, carry):
        sum_copy((me + k) % n_plane, me).start()
        return carry

    def end_sum(k, carry):
        peer = (me + k) % n_plane
        sum_copy(peer, me).wait_send()
        sum_copy(peer, peer).wait_recv()
        return carry

    lax.fori_loop(1, n_plane, start_sum, 0)
    lax.fori_loop(1, n_plane, end_sum, 0)

    square = jnp.zeros((rows, LANES), jnp.float32)
    for r in range(n_plane):
        square = square + summed[r] * summed[r]
    scale = 1.0 / (float(total - 1) * float(total - 1) * f_all)
    square = jnp.broadcast_to(jnp.sum(square).reshape(1, 1), (TILE, LANES)) * scale
    share = square + 0.5 * jnp.broadcast_to(tail[4:5, :], (TILE, LANES))
    loss_in[0] = share
    loss_copy = pltpu.make_async_remote_copy(
        src_ref=loss_in.at[0],
        dst_ref=loss_in.at[1],
        send_sem=loss_send,
        recv_sem=loss_recv,
        device_id=partner,
        device_id_type=MESH,
    )
    loss_copy.start()

    factors = []
    for v in range(2):
        halves = []
        for h in range(2):
            first = (v * 2 + h) * per_block
            block = jnp.concatenate([summed[first + q] for q in range(per_block)], axis=0)
            halves.append(block - tail[v * 2 + h:v * 2 + h + 1, :] / total)
        factor = jnp.concatenate(halves, axis=1) * (coef / (total - 1))
        one = factor.astype(jnp.bfloat16)
        rest = factor - one.astype(jnp.float32)
        two = rest.astype(jnp.bfloat16)
        three = (rest - two.astype(jnp.float32)).astype(jnp.bfloat16)
        factors.append(jnp.concatenate([one, two, three], axis=0))

    def give_chunk(c, carry):
        cols = pl.ds(pl.multiple_of(c * width, width), width)
        results = []
        mine = [views[v][:, cols].astype(jnp.float32) for v in range(2)]
        gap = mine[0] - mine[1]
        for v in range(2):
            pull = jnp.dot(factors[v], cent[v, :, cols], preferred_element_type=jnp.float32)
            pull = pull[0:n_dev] + pull[n_dev:total] + pull[total:total + n_dev]
            kept = cent[v, 0:n_dev, cols].astype(jnp.float32)
            pull = pull - stats[v, 2:3, cols] * (kept - stats[v, 3:4, cols])
            results.append(pull - stats[v, 1:2, cols] * (mine[v] - stats[v, 0:1, cols]))
        grad_a[:, cols] = gap + results[0]
        grad_b[:, cols] = results[1] - gap
        return carry

    lax.fori_loop(0, n_chunks, give_chunk, 0)
    loss_copy.wait()
    loss_out[...] = (loss_in[0] + loss_in[1]) * (total / (50.0 * f_all))


def on_device(view_a, view_b):
    n_row = lax.axis_size("row")
    n_col = lax.axis_size("col")
    n_plane = n_row * n_col
    n_dev, shard = view_a.shape
    rows = 4 * n_dev // n_plane
    fits = n_dev == LANES and rows % TILE == 0 and n_dev % rows == 0
    if lax.axis_size("dp") != 2 or not fits or shard % LANES:
        return plain(view_a, view_b)
    total = 2 * n_dev
    n_chunks = 4 if shard % (4 * LANES) == 0 else 1
    width = shard // n_chunks
    space = pl.BlockSpec(memory_space=pltpu.VMEM)
    grad = jax.ShapeDtypeStruct((n_dev, shard), jnp.float32)
    grad_a, grad_b, loss = pl.pallas_call(
        functools.partial(gram_kernel, n_row, n_col),
        out_shape=(grad, grad, jax.ShapeDtypeStruct((TILE, LANES), jnp.float32)),
        in_specs=[space] * 2,
        out_specs=(space,) * 3,
        scratch_shapes=[
            pltpu.VMEM((n_chunks, 2, n_dev, width), jnp.bfloat16),
            pltpu.VMEM((2, total, shard), jnp.bfloat16),
            pltpu.VMEM((2, TILE, shard), jnp.float32),
            pltpu.VMEM((2, n_dev, total), jnp.float32),
            pltpu.VMEM((2, 16, total), jnp.float32),
            pltpu.VMEM((1, width), jnp.float32),
            pltpu.VMEM((n_plane, rows + TILE, LANES), jnp.float32),
            pltpu.VMEM((n_plane, rows + TILE, LANES), jnp.float32),
            pltpu.VMEM((n_plane, rows, LANES), jnp.float32),
            pltpu.VMEM((2, TILE, LANES), jnp.float32),
            pltpu.SemaphoreType.DMA((n_chunks, 2)),
            pltpu.SemaphoreType.DMA((n_chunks, 2)),
            pltpu.SemaphoreType.DMA((n_plane,)),
            pltpu.SemaphoreType.DMA((n_plane,)),
            pltpu.SemaphoreType.DMA((n_plane,)),
            pltpu.SemaphoreType.DMA((n_plane,)),
            pltpu.SemaphoreType.DMA,
            pltpu.SemaphoreType.DMA,
        ],
        compiler_params=pltpu.CompilerParams(
            collective_id=0, has_side_effects=True, vmem_limit_bytes=32 * 1024 * 1024
        ),
    )(view_a, view_b)
    return (grad_a, grad_b, loss[0, 0])


def solution(mesh):
    in_specs = (P("dp", ("row", "col")), P("dp", ("row", "col")))
    out_specs = (P("dp", ("row", "col")), P("dp", ("row", "col")), P())
    return jax.shard_map(
        on_device, mesh=mesh, in_specs=in_specs, out_specs=out_specs, check_vma=False
    )
```

```python
import functools

import jax
import jax.numpy as jnp
from jax import lax
from jax.experimental import pallas as pl
from jax.experimental.pallas import tpu as pltpu
from jax.sharding import PartitionSpec as P

LANES = 128
TILE = 8
MESH = pl.DeviceIdType.MESH


def plain(view_a, view_b):
    n_dp = lax.axis_size("dp")
    n_parts = lax.axis_size("row") * lax.axis_size("col")
    dp_index = lax.axis_index("dp")
    n_dev, shard = view_a.shape
    total = n_dev * n_dp
    f_all = shard * n_parts
    coef = 2.0 * total / (25.0 * (total - 1))
    share = shard // n_dp

    own = jnp.stack([view_a, view_b])
    full = lax.all_gather(own, "dp", axis=1, tiled=True).astype(jnp.float32)
    mean = jnp.sum(full, axis=1, keepdims=True) / total
    diff = full - mean
    std = jnp.sqrt(jnp.sum(diff * diff, axis=1, keepdims=True) / (total - 1) + 0.0001)
    cent = diff.astype(jnp.bfloat16)
    cent32 = cent.astype(jnp.float32)
    diag = jnp.sum(cent32 * cent32, axis=1, keepdims=True) / (total - 1)

    piece = lax.dynamic_slice_in_dim(cent, dp_index * share, share, 2)
    gram = lax.dot_general(
        piece, piece, (((2,), (2,)), ((0,), (0,))), preferred_element_type=jnp.float32
    )
    own32 = own.astype(jnp.float32)
    gap = own32[0] - own32[1]
    local = 25.0 * jnp.sum(gap * gap) / (total * f_all)
    per_feature = 25.0 * jnp.maximum(1.0 - std, 0.0) - diag * diag
    local = local + jnp.sum(per_feature) / (f_all * n_dp)
    gram, local = lax.psum((gram, local), ("dp", "row", "col"))
    gram = gram / (total - 1)
    objective = (local + jnp.sum(gram * gram) / f_all) * total / (50.0 * f_all)

    lean = gram - jnp.mean(gram, axis=1, keepdims=True)
    lean = lax.dynamic_slice_in_dim(lean, dp_index * n_dev, n_dev, 1)
    pull = lax.dot_general(
        lean,
        cent32,
        (((2,), (1,)), ((0,), (0,))),
        preferred_element_type=jnp.float32,
        precision=lax.Precision.HIGHEST,
    )
    mine = lax.dynamic_slice_in_dim(cent32, dp_index * n_dev, n_dev, 1)
    pull = pull - diag * (mine - jnp.mean(cent32, axis=1, keepdims=True))
    hinge = jnp.where(std < 1.0, total * (own32 - mean) / (2.0 * std * (total - 1)), 0.0)
    rest = coef * pull - hinge
    return (gap + rest[0], rest[1] - gap, objective)


def gram_kernel(
    n_row,
    n_col,
    view_a,
    view_b,
    grad_a,
    grad_b,
    loss_out,
    mine,
    other,
    cent,
    stats,
    sums,
    gram_own,
    gram_cross,
    extra,
    local,
    out_own,
    in_own,
    all_own,
    out_cross,
    in_cross,
    all_cross,
    pair,
    load_sem,
    view_send,
    view_recv,
    sums_sem,
    pair_sem,
    own_send,
    own_recv,
    own_all_send,
    own_all_recv,
    cross_send,
    cross_recv,
    cross_all_send,
    cross_all_recv,
):
    views = (view_a, view_b)
    grads = (grad_a, grad_b)
    n_dev, shard = view_a.shape
    total = 2 * n_dev
    n_plane = n_row * n_col
    f_all = shard * n_plane
    coef = 2.0 * total / (25.0 * (total - 1))
    n_chunks = other.shape[0]
    half = n_chunks // 2
    width = other.shape[3]
    rows = all_own.shape[1]
    dp = lax.axis_index("dp")
    me = lax.axis_index("row") * n_col + lax.axis_index("col")
    partner = {"dp": 1 - dp}

    def columns(c):
        return pl.ds(pl.multiple_of(c * width, width), width)

    def load(v, c):
        return pltpu.make_async_copy(
            views[v].at[:, columns(c)], mine.at[v, :, columns(c)], load_sem.at[c, v]
        )

    for c in range(n_chunks):
        load(0, c).start()
        load(1, c).start()

    def place(peer):
        return {"row": peer // n_col, "col": peer % n_col}

    barrier = pltpu.get_barrier_semaphore()
    pl.semaphore_signal(barrier, inc=1, device_id=partner, device_id_type=MESH)

    def greet(k, carry):
        peer = (me + k) % n_plane
        pl.semaphore_signal(barrier, inc=1, device_id=place(peer), device_id_type=MESH)
        return carry

    lax.fori_loop(1, n_plane, greet, 0)
    pl.semaphore_wait(barrier, n_plane)

    def to_partner(source, target, send_sem, recv_sem):
        return pltpu.make_async_remote_copy(
            src_ref=source,
            dst_ref=target,
            send_sem=send_sem,
            recv_sem=recv_sem,
            device_id=partner,
            device_id_type=MESH,
        )

    def view_copy(v, c):
        return to_partner(
            views[v].at[:, columns(c)], other.at[c, v], view_send.at[c, v], view_recv.at[c, v]
        )

    def send_views(k, carry):
        c = (half * (1 - dp) + k) % n_chunks
        view_copy(0, c).start()
        view_copy(1, c).start()
        return carry

    lax.fori_loop(0, 1, send_views, 0)

    def add_rows(x):
        return jnp.sum(x, axis=0, keepdims=True)

    def own_sums(c, carry):
        for v in range(2):
            load(v, c).wait()
            sums[0, v:v + 1, columns(c)] = add_rows(mine[v, :, columns(c)].astype(jnp.float32))
        return carry

    lax.fori_loop(0, n_chunks, own_sums, 0)
    sums_copy = to_partner(sums.at[0], sums.at[1], sums_sem.at[0], sums_sem.at[1])
    sums_copy.start()
    lax.fori_loop(1, n_chunks, send_views, 0)
    gram_own[...] = jnp.zeros_like(gram_own)
    gram_cross[...] = jnp.zeros_like(gram_cross)
    extra[...] = jnp.zeros_like(extra)
    local[...] = jnp.zeros_like(local)
    sums_copy.wait()
    dims = (((1,), (1,)), ((), ()))

    def center_own(c, carry):
        cols = columns(c)
        for v in range(2):
            mean = (sums[0, v:v + 1, cols] + sums[1, v:v + 1, cols]) / total
            diff = mine[v, :, cols].astype(jnp.float32) - mean
            kept = diff.astype(jnp.bfloat16)
            cent[v, dp, :, cols] = kept
            back = kept.astype(jnp.float32)
            stats[v, 0:1, cols] = mean
            stats[v, 4:5, cols] = add_rows(diff * diff)
            stats[v, 5:6, cols] = add_rows(back * back)
            stats[v, 6:7, cols] = add_rows(back)
            gram_own[v] += lax.dot_general(kept, kept, dims, preferred_element_type=jnp.float32)
        return carry

    lax.fori_loop(0, n_chunks, center_own, 0)

    def exchange(source, target, send_sem, recv_sem, scatter):
        def copy(peer, slot):
            return pltpu.make_async_remote_copy(
                src_ref=source.at[peer if scatter else slot],
                dst_ref=target.at[slot],
                send_sem=send_sem.at[peer],
                recv_sem=recv_sem.at[slot],
                device_id=place(peer),
                device_id_type=MESH,
            )

        def start_one(k, carry):
            copy((me + k) % n_plane, me).start()
            return carry

        def end_one(k, carry):
            peer = (me + k) % n_plane
            copy(peer, me).wait_send()
            copy(peer, peer).wait_recv()
            return carry

        def start():
            lax.fori_loop(1, n_plane, start_one, 0)

        def end():
            lax.fori_loop(1, n_plane, end_one, 0)

        return start, end

    def added(ref):
        piece = ref[0]
        for r in range(1, n_plane):
            piece = piece + ref[r]
        return piece

    start_own, end_own = exchange(out_own, in_own, own_send, own_recv, True)
    start_own_all, end_own_all = exchange(all_own, all_own, own_all_send, own_all_recv, False)
    start_cross, end_cross = exchange(out_cross, in_cross, cross_send, cross_recv, True)
    start_cross_all, end_cross_all = exchange(
        all_cross, all_cross, cross_all_send, cross_all_recv, False
    )
    per_block = n_dev // rows
    for r in range(n_plane):
        first = r % per_block * rows
        out_own[r] = gram_own[r // per_block, first:first + rows, :]
    start_own()
    in_own[me] = out_own[me]

    def take_chunk(k, multiply):
        c = (half * dp + k) % n_chunks
        cols = columns(c)
        both = [mine[v, :, cols].astype(jnp.float32) for v in range(2)]
        gap = both[0] - both[1]
        for v in range(2):
            view_copy(v, c).wait_recv()
            mean = stats[v, 0:1, cols]
            diff = other[c, v].astype(jnp.float32) - mean
            kept = diff.astype(jnp.bfloat16)
            cent[v, 1 - dp, :, cols] = kept
            back = kept.astype(jnp.float32)
            std = jnp.sqrt((stats[v, 4:5, cols] + add_rows(diff * diff)) / (total - 1) + 0.0001)
            diag = (stats[v, 5:6, cols] + add_rows(back * back)) / (total - 1)
            column = stats[v, 6:7, cols] + add_rows(back)
            slope = jnp.where(std < 1.0, total / (2.0 * std * (total - 1)), 0.0)
            own = cent[v, dp, :, cols].astype(jnp.float32)
            rest = slope * (both[v] - mean) + (coef * diag) * (own - column / total)
            grads[v][:, cols] = (gap if v == 0 else -gap) - rest
            if multiply:
                local[...] += (25.0 * jnp.maximum(1.0 - std, 0.0) - diag * diag) / f_all
                high = column.astype(jnp.bfloat16).astype(jnp.float32)
                row = lax.broadcasted_iota(jnp.int32, (16, width), 0)
                parts = jnp.where(row == 0, high, jnp.where(row == 1, column - high, 0.0))
                gram_cross[v] += lax.dot_general(
                    cent[v, 0, :, cols],
                    cent[v, 1, :, cols],
                    dims,
                    preferred_element_type=jnp.float32,
                )
                for h in range(2):
                    extra[v, h] += lax.dot_general(
                        parts.astype(jnp.bfloat16),
                        cent[v, h, :, cols],
                        dims,
                        preferred_element_type=jnp.float32,
                    )
        if multiply:
            gap_other = other[c, 0].astype(jnp.float32) - other[c, 1].astype(jnp.float32)
            squares = add_rows(gap * gap) + add_rows(gap_other * gap_other)
            local[...] += 25.0 * squares / (total * f_all)

    take_chunk(0, True)
    end_own()
    all_own[me] = added(in_own)
    start_own_all()
    for k in range(1, half):
        take_chunk(k, True)

    local_sum = jnp.broadcast_to(jnp.sum(local[...]).reshape(1, 1), (1, LANES))
    tail = jnp.concatenate(
        [add_rows(extra[v, h]) for v in range(2) for h in range(2)]
        + [local_sum, jnp.zeros((TILE - 5, LANES), jnp.float32)],
        axis=0,
    )
    for r in range(n_plane):
        first = r % per_block * rows
        out_cross[r, 0:rows, :] = gram_cross[r // per_block, first:first + rows, :]
        out_cross[r, rows:rows + TILE, :] = tail
    start_cross()
    in_cross[me] = out_cross[me]
    end_own_all()

    def squared(ref):
        square = jnp.zeros((rows, LANES), jnp.float32)
        for r in range(n_plane):
            square = square + ref[r] * ref[r]
        return jnp.broadcast_to(jnp.sum(square).reshape(1, 1), (1, LANES))

    own_square = squared(all_own)
    end_cross()
    piece = added(in_cross)
    pair[0] = piece
    pair[0, rows + 5:rows + 6, :] = own_square
    pair_copy = to_partner(pair.at[0], pair.at[1], pair_sem.at[0], pair_sem.at[1])
    pair_copy.start()
    for k in range(half, n_chunks - 1):
        take_chunk(k, False)
    pair_copy.wait()
    piece = pair[0] + pair[1]
    all_cross[me] = piece[0:rows, :]
    start_cross_all()
    tail = piece[rows:rows + TILE, :]
    end_cross_all()

    first_half = jnp.full((n_dev, LANES), dp, jnp.int32) == 0
    factors = []
    for v in range(2):
        span = range(v * per_block, (v + 1) * per_block)
        own = jnp.concatenate([all_own[r] for r in span], axis=0)
        cross = jnp.concatenate([all_cross[r] for r in span], axis=0)
        left = jnp.where(first_half, own, cross.T) - tail[2 * v:2 * v + 1, :] / total
        right = jnp.where(first_half, cross, own) - tail[2 * v + 1:2 * v + 2, :] / total
        factor = jnp.concatenate([left, right], axis=1) * (coef / (total - 1))
        one = factor.astype(jnp.bfloat16)
        rest = factor - one.astype(jnp.float32)
        two = rest.astype(jnp.bfloat16)
        three = (rest - two.astype(jnp.float32)).astype(jnp.bfloat16)
        factors.append(jnp.concatenate([one, two, three], axis=0))

    def give_chunk(k, carry):
        cols = columns((half * dp + k) % n_chunks)
        for v in range(2):
            right = cent[v, :, :, cols].reshape(total, width)
            pull = jnp.dot(factors[v], right, preferred_element_type=jnp.float32)
            grads[v][:, cols] += pull[0:n_dev] + pull[n_dev:total] + pull[total:total + n_dev]
        return carry

    lax.fori_loop(0, n_chunks - 1, give_chunk, 0)
    square = tail[5:6, :] + 2.0 * squared(all_cross)
    loss = tail[4:5, :] + square / (float(total - 1) * float(total - 1) * f_all)
    loss_out[...] = jnp.broadcast_to(loss * (total / (50.0 * f_all)), (TILE, LANES))
    take_chunk(n_chunks - 1, False)
    give_chunk(n_chunks - 1, 0)

    def end_views(c, carry):
        view_copy(0, c).wait_send()
        view_copy(1, c).wait_send()
        return carry

    lax.fori_loop(0, n_chunks, end_views, 0)


def on_device(view_a, view_b):
    n_row = lax.axis_size("row")
    n_col = lax.axis_size("col")
    n_plane = n_row * n_col
    n_dev, shard = view_a.shape
    total = 2 * n_dev
    rows = total // n_plane
    n_chunks = 4
    width = shard // n_chunks
    fits = n_dev == LANES and rows > 0 and rows % TILE == 0 and n_dev % rows == 0
    if lax.axis_size("dp") != 2 or not fits or shard % (n_chunks * LANES):
        return plain(view_a, view_b)
    space = pl.BlockSpec(memory_space=pltpu.VMEM)
    grad = jax.ShapeDtypeStruct((n_dev, shard), jnp.float32)
    own_part = pltpu.VMEM((n_plane, rows, LANES), jnp.float32)
    cross_part = pltpu.VMEM((n_plane, rows + TILE, LANES), jnp.float32)
    plane_sems = pltpu.SemaphoreType.DMA((n_plane,))
    chunk_sems = pltpu.SemaphoreType.DMA((n_chunks, 2))
    pair_sems = pltpu.SemaphoreType.DMA((2,))
    grad_a, grad_b, loss = pl.pallas_call(
        functools.partial(gram_kernel, n_row, n_col),
        out_shape=(grad, grad, jax.ShapeDtypeStruct((TILE, LANES), jnp.float32)),
        in_specs=[pl.BlockSpec(memory_space=pl.ANY)] * 2,
        out_specs=(space,) * 3,
        scratch_shapes=[
            pltpu.VMEM((2, n_dev, shard), jnp.bfloat16),
            pltpu.VMEM((n_chunks, 2, n_dev, width), jnp.bfloat16),
            pltpu.VMEM((2, 2, n_dev, shard), jnp.bfloat16),
            pltpu.VMEM((2, TILE, shard), jnp.float32),
            pltpu.VMEM((2, 2, shard), jnp.float32),
            pltpu.VMEM((2, n_dev, LANES), jnp.float32),
            pltpu.VMEM((2, n_dev, LANES), jnp.float32),
            pltpu.VMEM((2, 2, 16, LANES), jnp.float32),
            pltpu.VMEM((1, width), jnp.float32),
            own_part,
            own_part,
            own_part,
            cross_part,
            cross_part,
            own_part,
            pltpu.VMEM((2, rows + TILE, LANES), jnp.float32),
            chunk_sems,
            chunk_sems,
            chunk_sems,
            pair_sems,
            pair_sems,
        ]
        + [plane_sems] * 8,
        compiler_params=pltpu.CompilerParams(
            collective_id=0, has_side_effects=True, vmem_limit_bytes=48 * 1024 * 1024
        ),
    )(view_a, view_b)
    return (grad_a, grad_b, loss[0, 0])


def solution(mesh):
    in_specs = (P("dp", ("row", "col")), P("dp", ("row", "col")))
    out_specs = (P("dp", ("row", "col")), P("dp", ("row", "col")), P())
    return jax.shard_map(
        on_device, mesh=mesh, in_specs=in_specs, out_specs=out_specs, check_vma=False
    )
```

```python
import functools

import jax
import jax.numpy as jnp
from jax import lax
from jax.experimental import pallas as pl
from jax.experimental.pallas import tpu as pltpu
from jax.sharding import PartitionSpec as P

LANES = 128
TILE = 8
MESH = pl.DeviceIdType.MESH


def plain(view_a, view_b):
    n_dp = lax.axis_size("dp")
    n_parts = lax.axis_size("row") * lax.axis_size("col")
    dp_index = lax.axis_index("dp")
    n_dev, shard = view_a.shape
    total = n_dev * n_dp
    f_all = shard * n_parts
    coef = 2.0 * total / (25.0 * (total - 1))
    share = shard // n_dp

    own = jnp.stack([view_a, view_b])
    full = lax.all_gather(own, "dp", axis=1, tiled=True).astype(jnp.float32)
    mean = jnp.sum(full, axis=1, keepdims=True) / total
    diff = full - mean
    std = jnp.sqrt(jnp.sum(diff * diff, axis=1, keepdims=True) / (total - 1) + 0.0001)
    cent = diff.astype(jnp.bfloat16)
    cent32 = cent.astype(jnp.float32)
    diag = jnp.sum(cent32 * cent32, axis=1, keepdims=True) / (total - 1)

    piece = lax.dynamic_slice_in_dim(cent, dp_index * share, share, 2)
    gram = lax.dot_general(
        piece, piece, (((2,), (2,)), ((0,), (0,))), preferred_element_type=jnp.float32
    )
    own32 = own.astype(jnp.float32)
    gap = own32[0] - own32[1]
    local = 25.0 * jnp.sum(gap * gap) / (total * f_all)
    per_feature = 25.0 * jnp.maximum(1.0 - std, 0.0) - diag * diag
    local = local + jnp.sum(per_feature) / (f_all * n_dp)
    gram, local = lax.psum((gram, local), ("dp", "row", "col"))
    gram = gram / (total - 1)
    objective = (local + jnp.sum(gram * gram) / f_all) * total / (50.0 * f_all)

    lean = gram - jnp.mean(gram, axis=1, keepdims=True)
    lean = lax.dynamic_slice_in_dim(lean, dp_index * n_dev, n_dev, 1)
    pull = lax.dot_general(
        lean,
        cent32,
        (((2,), (1,)), ((0,), (0,))),
        preferred_element_type=jnp.float32,
        precision=lax.Precision.HIGHEST,
    )
    mine = lax.dynamic_slice_in_dim(cent32, dp_index * n_dev, n_dev, 1)
    pull = pull - diag * (mine - jnp.mean(cent32, axis=1, keepdims=True))
    hinge = jnp.where(std < 1.0, total * (own32 - mean) / (2.0 * std * (total - 1)), 0.0)
    rest = coef * pull - hinge
    return (gap + rest[0], rest[1] - gap, objective)


def gram_kernel(
    n_row,
    n_col,
    view_a,
    view_b,
    grad_a,
    grad_b,
    loss_out,
    mine,
    other,
    cent,
    stats,
    sums,
    gram_own,
    gram_cross,
    extra,
    local,
    out_own,
    in_own,
    all_own,
    out_cross,
    in_cross,
    all_cross,
    pair,
    load_sem,
    view_send,
    view_recv,
    sums_sem,
    pair_sem,
    own_send,
    own_recv,
    own_all_send,
    own_all_recv,
    cross_send,
    cross_recv,
    cross_all_send,
    cross_all_recv,
):
    views = (view_a, view_b)
    grads = (grad_a, grad_b)
    n_dev, shard = view_a.shape
    total = 2 * n_dev
    n_plane = n_row * n_col
    f_all = shard * n_plane
    coef = 2.0 * total / (25.0 * (total - 1))
    n_chunks = other.shape[0]
    half = n_chunks // 2
    held = 2
    width = other.shape[3]
    rows = all_own.shape[1]
    dp = lax.axis_index("dp")
    me = lax.axis_index("row") * n_col + lax.axis_index("col")
    partner = {"dp": 1 - dp}

    def columns(c):
        return pl.ds(pl.multiple_of(c * width, width), width)

    def load(v, c):
        return pltpu.make_async_copy(
            views[v].at[:, columns(c)], mine.at[v, :, columns(c)], load_sem.at[c, v]
        )

    for c in range(n_chunks):
        load(0, c).start()
        load(1, c).start()

    def place(peer):
        return {"row": peer // n_col, "col": peer % n_col}

    barrier = pltpu.get_barrier_semaphore()
    pl.semaphore_signal(barrier, inc=1, device_id=partner, device_id_type=MESH)

    def greet(k, carry):
        peer = (me + k) % n_plane
        pl.semaphore_signal(barrier, inc=1, device_id=place(peer), device_id_type=MESH)
        return carry

    lax.fori_loop(1, n_plane, greet, 0)
    pl.semaphore_wait(barrier, n_plane)

    def to_partner(source, target, send_sem, recv_sem):
        return pltpu.make_async_remote_copy(
            src_ref=source,
            dst_ref=target,
            send_sem=send_sem,
            recv_sem=recv_sem,
            device_id=partner,
            device_id_type=MESH,
        )

    def view_copy(v, c):
        return to_partner(
            views[v].at[:, columns(c)], other.at[c, v], view_send.at[c, v], view_recv.at[c, v]
        )

    def send_views(k, carry):
        c = (half * (1 - dp) + k) % n_chunks
        view_copy(0, c).start()
        view_copy(1, c).start()
        return carry

    lax.fori_loop(0, 1, send_views, 0)

    def add_rows(x):
        return jnp.sum(x, axis=0, keepdims=True)

    def own_sums(c, carry):
        for v in range(2):
            load(v, c).wait()
            sums[0, v:v + 1, columns(c)] = add_rows(mine[v, :, columns(c)].astype(jnp.float32))
        return carry

    lax.fori_loop(0, n_chunks, own_sums, 0)
    sums_copy = to_partner(sums.at[0], sums.at[1], sums_sem.at[0], sums_sem.at[1])
    sums_copy.start()
    lax.fori_loop(1, n_chunks - held, send_views, 0)
    gram_own[...] = jnp.zeros_like(gram_own)
    gram_cross[...] = jnp.zeros_like(gram_cross)
    extra[...] = jnp.zeros_like(extra)
    local[...] = jnp.zeros_like(local)
    sums_copy.wait()
    dims = (((1,), (1,)), ((), ()))

    def center_own(c, carry):
        cols = columns(c)
        for v in range(2):
            mean = (sums[0, v:v + 1, cols] + sums[1, v:v + 1, cols]) / total
            diff = mine[v, :, cols].astype(jnp.float32) - mean
            kept = diff.astype(jnp.bfloat16)
            cent[v, dp, :, cols] = kept
            back = kept.astype(jnp.float32)
            stats[v, 0:1, cols] = mean
            stats[v, 4:5, cols] = add_rows(diff * diff)
            stats[v, 5:6, cols] = add_rows(back * back)
            stats[v, 6:7, cols] = add_rows(back)
            gram_own[v] += lax.dot_general(kept, kept, dims, preferred_element_type=jnp.float32)
        return carry

    lax.fori_loop(0, n_chunks, center_own, 0)

    def exchange(source, target, send_sem, recv_sem, scatter):
        def copy(peer, slot):
            return pltpu.make_async_remote_copy(
                src_ref=source.at[peer if scatter else slot],
                dst_ref=target.at[slot],
                send_sem=send_sem.at[peer],
                recv_sem=recv_sem.at[slot],
                device_id=place(peer),
                device_id_type=MESH,
            )

        def start_one(k, carry):
            copy((me + k) % n_plane, me).start()
            return carry

        def end_one(k, carry):
            peer = (me + k) % n_plane
            copy(peer, me).wait_send()
            copy(peer, peer).wait_recv()
            return carry

        def start():
            lax.fori_loop(1, n_plane, start_one, 0)

        def end():
            lax.fori_loop(1, n_plane, end_one, 0)

        return start, end

    def added(ref):
        piece = ref[0]
        for r in range(1, n_plane):
            piece = piece + ref[r]
        return piece

    start_own, end_own = exchange(out_own, in_own, own_send, own_recv, True)
    start_own_all, end_own_all = exchange(all_own, all_own, own_all_send, own_all_recv, False)
    start_cross, end_cross = exchange(out_cross, in_cross, cross_send, cross_recv, True)
    start_cross_all, end_cross_all = exchange(
        all_cross, all_cross, cross_all_send, cross_all_recv, False
    )
    per_block = n_dev // rows
    for r in range(n_plane):
        first = r % per_block * rows
        out_own[r] = gram_own[r // per_block, first:first + rows, :]
    start_own()
    in_own[me] = out_own[me]

    def take_chunk(k, multiply):
        c = (half * dp + k) % n_chunks
        cols = columns(c)
        both = [mine[v, :, cols].astype(jnp.float32) for v in range(2)]
        gap = both[0] - both[1]
        for v in range(2):
            view_copy(v, c).wait_recv()
            mean = stats[v, 0:1, cols]
            diff = other[c, v].astype(jnp.float32) - mean
            kept = diff.astype(jnp.bfloat16)
            cent[v, 1 - dp, :, cols] = kept
            back = kept.astype(jnp.float32)
            std = jnp.sqrt((stats[v, 4:5, cols] + add_rows(diff * diff)) / (total - 1) + 0.0001)
            diag = (stats[v, 5:6, cols] + add_rows(back * back)) / (total - 1)
            column = stats[v, 6:7, cols] + add_rows(back)
            slope = jnp.where(std < 1.0, total / (2.0 * std * (total - 1)), 0.0)
            own = cent[v, dp, :, cols].astype(jnp.float32)
            rest = slope * (both[v] - mean) + (coef * diag) * (own - column / total)
            grads[v][:, cols] = (gap if v == 0 else -gap) - rest
            if multiply:
                local[...] += (25.0 * jnp.maximum(1.0 - std, 0.0) - diag * diag) / f_all
                high = column.astype(jnp.bfloat16).astype(jnp.float32)
                row = lax.broadcasted_iota(jnp.int32, (16, width), 0)
                parts = jnp.where(row == 0, high, jnp.where(row == 1, column - high, 0.0))
                gram_cross[v] += lax.dot_general(
                    cent[v, 0, :, cols],
                    cent[v, 1, :, cols],
                    dims,
                    preferred_element_type=jnp.float32,
                )
                for h in range(2):
                    extra[v, h] += lax.dot_general(
                        parts.astype(jnp.bfloat16),
                        cent[v, h, :, cols],
                        dims,
                        preferred_element_type=jnp.float32,
                    )
        if multiply:
            gap_other = other[c, 0].astype(jnp.float32) - other[c, 1].astype(jnp.float32)
            squares = add_rows(gap * gap) + add_rows(gap_other * gap_other)
            local[...] += 25.0 * squares / (total * f_all)

    def take_chunks(first, last, multiply):
        def one(k, carry):
            take_chunk(k, multiply)
            return carry

        lax.fori_loop(first, last, one, 0)

    take_chunks(0, 1, True)
    end_own()
    all_own[me] = added(in_own)
    start_own_all()
    take_chunks(1, half, True)

    local_sum = jnp.broadcast_to(jnp.sum(local[...]).reshape(1, 1), (1, LANES))
    tail = jnp.concatenate(
        [add_rows(extra[v, h]) for v in range(2) for h in range(2)]
        + [local_sum, jnp.zeros((TILE - 5, LANES), jnp.float32)],
        axis=0,
    )
    for r in range(n_plane):
        first = r % per_block * rows
        out_cross[r, 0:rows, :] = gram_cross[r // per_block, first:first + rows, :]
        out_cross[r, rows:rows + TILE, :] = tail
    start_cross()
    in_cross[me] = out_cross[me]
    end_own_all()

    def squared(ref):
        square = jnp.zeros((rows, LANES), jnp.float32)
        for r in range(n_plane):
            square = square + ref[r] * ref[r]
        return jnp.broadcast_to(jnp.sum(square).reshape(1, 1), (1, LANES))

    own_square = squared(all_own)
    take_chunks(half, half + 1, False)
    end_cross()
    piece = added(in_cross)
    pair[0] = piece
    pair[0, rows + 5:rows + 6, :] = own_square
    pair_copy = to_partner(pair.at[0], pair.at[1], pair_sem.at[0], pair_sem.at[1])
    pair_copy.start()
    lax.fori_loop(n_chunks - held, n_chunks, send_views, 0)
    take_chunks(half + 1, n_chunks - held, False)
    pair_copy.wait()
    piece = pair[0] + pair[1]
    all_cross[me] = piece[0:rows, :]
    start_cross_all()
    tail = piece[rows:rows + TILE, :]
    take_chunks(n_chunks - held, n_chunks - 1, False)
    end_cross_all()

    first_half = jnp.full((n_dev, LANES), dp, jnp.int32) == 0
    factors = []
    for v in range(2):
        span = range(v * per_block, (v + 1) * per_block)
        own = jnp.concatenate([all_own[r] for r in span], axis=0)
        cross = jnp.concatenate([all_cross[r] for r in span], axis=0)
        left = jnp.where(first_half, own, cross.T) - tail[2 * v:2 * v + 1, :] / total
        right = jnp.where(first_half, cross, own) - tail[2 * v + 1:2 * v + 2, :] / total
        factor = jnp.concatenate([left, right], axis=1) * (coef / (total - 1))
        one = factor.astype(jnp.bfloat16)
        rest = factor - one.astype(jnp.float32)
        two = rest.astype(jnp.bfloat16)
        three = (rest - two.astype(jnp.float32)).astype(jnp.bfloat16)
        factors.append(jnp.concatenate([one, two, three], axis=0))

    def give_chunk(k, carry):
        cols = columns((half * dp + k) % n_chunks)
        for v in range(2):
            right = cent[v, :, :, cols].reshape(total, width)
            pull = jnp.dot(factors[v], right, preferred_element_type=jnp.float32)
            grads[v][:, cols] += pull[0:n_dev] + pull[n_dev:total] + pull[total:total + n_dev]
        return carry

    lax.fori_loop(0, n_chunks - 1, give_chunk, 0)
    square = tail[5:6, :] + 2.0 * squared(all_cross)
    loss = tail[4:5, :] + square / (float(total - 1) * float(total - 1) * f_all)
    loss_out[...] = loss[0:1, 0:1] * (total / (50.0 * f_all))
    take_chunks(n_chunks - 1, n_chunks, False)
    lax.fori_loop(n_chunks - 1, n_chunks, give_chunk, 0)

    def end_views(c, carry):
        view_copy(0, c).wait_send()
        view_copy(1, c).wait_send()
        return carry

    lax.fori_loop(0, n_chunks, end_views, 0)


def on_device(view_a, view_b):
    n_row = lax.axis_size("row")
    n_col = lax.axis_size("col")
    n_plane = n_row * n_col
    n_dev, shard = view_a.shape
    total = 2 * n_dev
    rows = total // n_plane
    n_chunks = 8
    width = shard // n_chunks
    fits = n_dev == LANES and rows > 0 and rows % TILE == 0 and n_dev % rows == 0
    if lax.axis_size("dp") != 2 or not fits or shard % (n_chunks * LANES):
        return plain(view_a, view_b)
    space = pl.BlockSpec(memory_space=pltpu.VMEM)
    grad = jax.ShapeDtypeStruct((n_dev, shard), jnp.float32)
    own_part = pltpu.VMEM((n_plane, rows, LANES), jnp.float32)
    cross_part = pltpu.VMEM((n_plane, rows + TILE, LANES), jnp.float32)
    plane_sems = pltpu.SemaphoreType.DMA((n_plane,))
    chunk_sems = pltpu.SemaphoreType.DMA((n_chunks, 2))
    pair_sems = pltpu.SemaphoreType.DMA((2,))
    grad_a, grad_b, loss = pl.pallas_call(
        functools.partial(gram_kernel, n_row, n_col),
        out_shape=(grad, grad, jax.ShapeDtypeStruct((1, 1), jnp.float32)),
        in_specs=[pl.BlockSpec(memory_space=pltpu.HBM)] * 2,
        out_specs=(space,) * 3,
        scratch_shapes=[
            pltpu.VMEM((2, n_dev, shard), jnp.bfloat16),
            pltpu.VMEM((n_chunks, 2, n_dev, width), jnp.bfloat16),
            pltpu.VMEM((2, 2, n_dev, shard), jnp.bfloat16),
            pltpu.VMEM((2, TILE, shard), jnp.float32),
            pltpu.VMEM((2, 2, shard), jnp.float32),
            pltpu.VMEM((2, n_dev, LANES), jnp.float32),
            pltpu.VMEM((2, n_dev, LANES), jnp.float32),
            pltpu.VMEM((2, 2, 16, LANES), jnp.float32),
            pltpu.VMEM((1, width), jnp.float32),
            own_part,
            own_part,
            own_part,
            cross_part,
            cross_part,
            own_part,
            pltpu.VMEM((2, rows + TILE, LANES), jnp.float32),
            chunk_sems,
            chunk_sems,
            chunk_sems,
            pair_sems,
            pair_sems,
        ]
        + [plane_sems] * 8,
        compiler_params=pltpu.CompilerParams(
            collective_id=0, has_side_effects=True, vmem_limit_bytes=48 * 1024 * 1024
        ),
    )(view_a, view_b)
    return (grad_a, grad_b, loss.reshape(()))


def solution(mesh):
    in_specs = (P("dp", ("row", "col")), P("dp", ("row", "col")))
    out_specs = (P("dp", ("row", "col")), P("dp", ("row", "col")), P())
    return jax.shard_map(
        on_device, mesh=mesh, in_specs=in_specs, out_specs=out_specs, check_vma=False
    )
```

```python
import functools

import jax
import jax.numpy as jnp
from jax import lax
from jax.experimental import pallas as pl
from jax.experimental.pallas import tpu as pltpu
from jax.sharding import PartitionSpec as P

LANES = 128
TILE = 8
MESH = pl.DeviceIdType.MESH


def plain(view_a, view_b):
    n_dp = lax.axis_size("dp")
    n_parts = lax.axis_size("row") * lax.axis_size("col")
    dp_index = lax.axis_index("dp")
    n_dev, shard = view_a.shape
    total = n_dev * n_dp
    f_all = shard * n_parts
    coef = 2.0 * total / (25.0 * (total - 1))
    share = shard // n_dp

    own = jnp.stack([view_a, view_b])
    full = lax.all_gather(own, "dp", axis=1, tiled=True).astype(jnp.float32)
    mean = jnp.sum(full, axis=1, keepdims=True) / total
    diff = full - mean
    std = jnp.sqrt(jnp.sum(diff * diff, axis=1, keepdims=True) / (total - 1) + 0.0001)
    cent = diff.astype(jnp.bfloat16)
    cent32 = cent.astype(jnp.float32)
    diag = jnp.sum(cent32 * cent32, axis=1, keepdims=True) / (total - 1)

    piece = lax.dynamic_slice_in_dim(cent, dp_index * share, share, 2)
    gram = lax.dot_general(
        piece, piece, (((2,), (2,)), ((0,), (0,))), preferred_element_type=jnp.float32
    )
    own32 = own.astype(jnp.float32)
    gap = own32[0] - own32[1]
    local = 25.0 * jnp.sum(gap * gap) / (total * f_all)
    per_feature = 25.0 * jnp.maximum(1.0 - std, 0.0) - diag * diag
    local = local + jnp.sum(per_feature) / (f_all * n_dp)
    gram, local = lax.psum((gram, local), ("dp", "row", "col"))
    gram = gram / (total - 1)
    objective = (local + jnp.sum(gram * gram) / f_all) * total / (50.0 * f_all)

    lean = gram - jnp.mean(gram, axis=1, keepdims=True)
    lean = lax.dynamic_slice_in_dim(lean, dp_index * n_dev, n_dev, 1)
    pull = lax.dot_general(
        lean,
        cent32,
        (((2,), (1,)), ((0,), (0,))),
        preferred_element_type=jnp.float32,
        precision=lax.Precision.HIGHEST,
    )
    mine = lax.dynamic_slice_in_dim(cent32, dp_index * n_dev, n_dev, 1)
    pull = pull - diag * (mine - jnp.mean(cent32, axis=1, keepdims=True))
    hinge = jnp.where(std < 1.0, total * (own32 - mean) / (2.0 * std * (total - 1)), 0.0)
    rest = coef * pull - hinge
    return (gap + rest[0], rest[1] - gap, objective)


def gram_kernel(
    n_row,
    n_col,
    view_a,
    view_b,
    grad_a,
    grad_b,
    loss_out,
    mine,
    other,
    cent,
    stats,
    sums,
    gram_own,
    gram_cross,
    local,
    out_own,
    in_own,
    all_own,
    out_cross,
    in_cross,
    all_cross,
    all_tail,
    pair,
    load_sem,
    view_send,
    view_recv,
    sums_sem,
    pair_sem,
    own_send,
    own_recv,
    own_all_send,
    own_all_recv,
    cross_send,
    cross_recv,
    cross_all_send,
    cross_all_recv,
    tail_send,
    tail_recv,
):
    views = (view_a, view_b)
    grads = (grad_a, grad_b)
    n_dev, shard = view_a.shape
    total = 2 * n_dev
    n_plane = n_row * n_col
    f_all = shard * n_plane
    coef = 2.0 * total / (25.0 * (total - 1))
    n_chunks = other.shape[0]
    half = n_chunks // 2
    held = 2
    width = other.shape[3]
    rows = all_own.shape[1]
    dp = lax.axis_index("dp")
    me = lax.axis_index("row") * n_col + lax.axis_index("col")
    partner = {"dp": 1 - dp}

    def columns(c):
        return pl.ds(pl.multiple_of(c * width, width), width)

    def load(v, c):
        return pltpu.make_async_copy(
            views[v].at[:, columns(c)], mine.at[v, :, columns(c)], load_sem.at[c, v]
        )

    for c in range(n_chunks):
        load(0, c).start()
        load(1, c).start()

    def place(peer):
        return {"row": peer // n_col, "col": peer % n_col}

    barrier = pltpu.get_barrier_semaphore()
    pl.semaphore_signal(barrier, inc=1, device_id=partner, device_id_type=MESH)

    def greet(k, carry):
        peer = (me + k) % n_plane
        pl.semaphore_signal(barrier, inc=1, device_id=place(peer), device_id_type=MESH)
        return carry

    lax.fori_loop(1, n_plane, greet, 0)
    pl.semaphore_wait(barrier, n_plane)

    def to_partner(source, target, send_sem, recv_sem):
        return pltpu.make_async_remote_copy(
            src_ref=source,
            dst_ref=target,
            send_sem=send_sem,
            recv_sem=recv_sem,
            device_id=partner,
            device_id_type=MESH,
        )

    def view_copy(v, c):
        return to_partner(
            views[v].at[:, columns(c)], other.at[c, v], view_send.at[c, v], view_recv.at[c, v]
        )

    def send_views(k, carry):
        c = (half * (1 - dp) + k) % n_chunks
        view_copy(0, c).start()
        view_copy(1, c).start()
        return carry

    lax.fori_loop(0, 1, send_views, 0)

    def add_rows(x):
        return jnp.sum(x, axis=0, keepdims=True)

    def own_sums(c, carry):
        for v in range(2):
            load(v, c).wait()
            sums[0, v:v + 1, columns(c)] = add_rows(mine[v, :, columns(c)].astype(jnp.float32))
        return carry

    lax.fori_loop(0, n_chunks, own_sums, 0)
    sums_copy = to_partner(sums.at[0], sums.at[1], sums_sem.at[0], sums_sem.at[1])
    sums_copy.start()
    lax.fori_loop(1, n_chunks - held, send_views, 0)
    gram_own[...] = jnp.zeros_like(gram_own)
    gram_cross[...] = jnp.zeros_like(gram_cross)
    local[...] = jnp.zeros_like(local)
    sums_copy.wait()
    dims = (((1,), (1,)), ((), ()))

    def center_own(c, carry):
        cols = columns(c)
        for v in range(2):
            mean = (sums[0, v:v + 1, cols] + sums[1, v:v + 1, cols]) / total
            diff = mine[v, :, cols].astype(jnp.float32) - mean
            kept = diff.astype(jnp.bfloat16)
            cent[v, dp, :, cols] = kept
            back = kept.astype(jnp.float32)
            stats[v, 0:1, cols] = mean
            stats[v, 4:5, cols] = add_rows(diff * diff)
            stats[v, 5:6, cols] = add_rows(back * back)
            stats[v, 6:7, cols] = add_rows(back)
            gram_own[v] += lax.dot_general(kept, kept, dims, preferred_element_type=jnp.float32)
        return carry

    lax.fori_loop(0, n_chunks, center_own, 0)

    def exchange(source, target, send_sem, recv_sem, scatter):
        def copy(peer, slot):
            return pltpu.make_async_remote_copy(
                src_ref=source.at[peer if scatter else slot],
                dst_ref=target.at[slot],
                send_sem=send_sem.at[peer],
                recv_sem=recv_sem.at[slot],
                device_id=place(peer),
                device_id_type=MESH,
            )

        def start_one(k, carry):
            copy((me + k) % n_plane, me).start()
            return carry

        def end_one(k, carry):
            peer = (me + k) % n_plane
            copy(peer, me).wait_send()
            copy(peer, peer).wait_recv()
            return carry

        def start():
            lax.fori_loop(1, n_plane, start_one, 0)

        def end():
            lax.fori_loop(1, n_plane, end_one, 0)

        return start, end

    def added(ref):
        piece = ref[0]
        for r in range(1, n_plane):
            piece = piece + ref[r]
        return piece

    start_own, end_own = exchange(out_own, in_own, own_send, own_recv, True)
    start_own_all, end_own_all = exchange(all_own, all_own, own_all_send, own_all_recv, False)
    start_cross, end_cross = exchange(out_cross, in_cross, cross_send, cross_recv, True)
    start_cross_all, end_cross_all = exchange(
        all_cross, all_cross, cross_all_send, cross_all_recv, False
    )
    start_tail, end_tail = exchange(all_tail, all_tail, tail_send, tail_recv, False)
    per_block = n_dev // rows
    for r in range(n_plane):
        first = r % per_block * rows
        out_own[r] = gram_own[r // per_block, first:first + rows, :]
    start_own()
    in_own[me] = out_own[me]

    def take_chunk(k, multiply):
        c = (half * dp + k) % n_chunks
        cols = columns(c)
        both = [mine[v, :, cols].astype(jnp.float32) for v in range(2)]
        gap = both[0] - both[1]
        for v in range(2):
            view_copy(v, c).wait_recv()
            mean = stats[v, 0:1, cols]
            diff = other[c, v].astype(jnp.float32) - mean
            kept = diff.astype(jnp.bfloat16)
            cent[v, 1 - dp, :, cols] = kept
            back = kept.astype(jnp.float32)
            std = jnp.sqrt((stats[v, 4:5, cols] + add_rows(diff * diff)) / (total - 1) + 0.0001)
            diag = (stats[v, 5:6, cols] + add_rows(back * back)) / (total - 1)
            column = stats[v, 6:7, cols] + add_rows(back)
            slope = jnp.where(std < 1.0, total / (2.0 * std * (total - 1)), 0.0)
            own = cent[v, dp, :, cols].astype(jnp.float32)
            rest = slope * (both[v] - mean) + (coef * diag) * (own - column / total)
            grads[v][:, cols] = (gap if v == 0 else -gap) - rest
            if multiply:
                local[...] += (25.0 * jnp.maximum(1.0 - std, 0.0) - diag * diag) / f_all
                gram_cross[v] += lax.dot_general(
                    cent[v, 0, :, cols],
                    cent[v, 1, :, cols],
                    dims,
                    preferred_element_type=jnp.float32,
                )
        if multiply:
            gap_other = other[c, 0].astype(jnp.float32) - other[c, 1].astype(jnp.float32)
            squares = add_rows(gap * gap) + add_rows(gap_other * gap_other)
            local[...] += 25.0 * squares / (total * f_all)

    def take_chunks(first, last, multiply):
        def one(k, carry):
            take_chunk(k, multiply)
            return carry

        lax.fori_loop(first, last, one, 0)

    take_chunks(0, 1, True)
    end_own()
    all_own[me] = added(in_own)
    start_own_all()
    take_chunks(1, half, True)

    for r in range(n_plane):
        first = r % per_block * rows
        out_cross[r] = gram_cross[r // per_block, first:first + rows, :]
    start_cross()
    in_cross[me] = out_cross[me]
    end_own_all()

    def squared(ref):
        square = jnp.zeros((rows, LANES), jnp.float32)
        for r in range(n_plane):
            square = square + ref[r] * ref[r]
        return jnp.broadcast_to(jnp.sum(square).reshape(1, 1), (1, LANES))

    def whole(ref, v):
        return jnp.concatenate([ref[v * per_block + q] for q in range(per_block)], axis=0)

    pair[0, rows:rows + TILE, :] = jnp.concatenate(
        [
            add_rows(whole(all_own, 0)),
            add_rows(whole(all_own, 1)),
            jnp.broadcast_to(jnp.sum(local[...]).reshape(1, 1), (1, LANES)),
            squared(all_own),
            jnp.zeros((TILE - 4, LANES), jnp.float32),
        ],
        axis=0,
    )
    take_chunks(half, half + 1, False)
    end_cross()
    pair[0, 0:rows, :] = added(in_cross)
    pair_copy = to_partner(pair.at[0], pair.at[1], pair_sem.at[0], pair_sem.at[1])
    pair_copy.start()
    lax.fori_loop(n_chunks - held, n_chunks, send_views, 0)
    take_chunks(half + 1, n_chunks - held, False)
    pair_copy.wait()
    piece = pair[0] + pair[1]
    all_cross[me] = piece[0:rows, :]
    all_tail[me] = piece[rows:rows + TILE, :]
    start_cross_all()
    start_tail()
    take_chunks(n_chunks - held, n_chunks - 1, False)
    end_cross_all()

    first_half = jnp.full((n_dev, LANES), dp, jnp.int32) == 0
    factors = []
    for v in range(2):
        own = whole(all_own, v)
        cross = whole(all_cross, v)
        flipped = cross.T
        rest = jnp.where(first_half, flipped, cross)
        own = own - (add_rows(own) + add_rows(rest)) / total
        rest = jnp.where(first_half, cross, flipped)
        rest = rest - (add_rows(rest) + pair[1, rows + v:rows + v + 1, :]) / total
        left = jnp.where(first_half, own, rest)
        right = jnp.where(first_half, rest, own)
        factor = jnp.concatenate([left, right], axis=1) * (coef / (total - 1))
        one = factor.astype(jnp.bfloat16)
        rest = factor - one.astype(jnp.float32)
        two = rest.astype(jnp.bfloat16)
        three = (rest - two.astype(jnp.float32)).astype(jnp.bfloat16)
        factors.append(jnp.concatenate([one, two, three], axis=0))

    def give_chunk(k, carry):
        cols = columns((half * dp + k) % n_chunks)
        for v in range(2):
            right = cent[v, :, :, cols].reshape(total, width)
            pull = jnp.dot(factors[v], right, preferred_element_type=jnp.float32)
            grads[v][:, cols] += pull[0:n_dev] + pull[n_dev:total] + pull[total:total + n_dev]
        return carry

    lax.fori_loop(0, n_chunks - 1, give_chunk, 0)
    take_chunks(n_chunks - 1, n_chunks, False)
    lax.fori_loop(n_chunks - 1, n_chunks, give_chunk, 0)

    end_tail()
    square = all_tail[me][3:4, :] + 2.0 * squared(all_cross)
    loss = added(all_tail)[2:3, :] + square / (float(total - 1) * float(total - 1) * f_all)
    loss_out[...] = loss[0:1, 0:1] * (total / (50.0 * f_all))

    def end_views(c, carry):
        view_copy(0, c).wait_send()
        view_copy(1, c).wait_send()
        return carry

    lax.fori_loop(0, n_chunks, end_views, 0)


def on_device(view_a, view_b):
    n_row = lax.axis_size("row")
    n_col = lax.axis_size("col")
    n_plane = n_row * n_col
    n_dev, shard = view_a.shape
    total = 2 * n_dev
    rows = total // n_plane
    n_chunks = 8
    width = shard // n_chunks
    fits = n_dev == LANES and rows > 0 and rows % TILE == 0 and n_dev % rows == 0
    if lax.axis_size("dp") != 2 or not fits or shard % (n_chunks * LANES):
        return plain(view_a, view_b)
    space = pl.BlockSpec(memory_space=pltpu.VMEM)
    grad = jax.ShapeDtypeStruct((n_dev, shard), jnp.float32)
    view_a = pltpu.with_memory_space_constraint(view_a, pltpu.HBM)
    view_b = pltpu.with_memory_space_constraint(view_b, pltpu.HBM)
    own_part = pltpu.VMEM((n_plane, rows, LANES), jnp.float32)
    plane_sems = pltpu.SemaphoreType.DMA((n_plane,))
    chunk_sems = pltpu.SemaphoreType.DMA((n_chunks, 2))
    pair_sems = pltpu.SemaphoreType.DMA((2,))
    grad_a, grad_b, loss = pl.pallas_call(
        functools.partial(gram_kernel, n_row, n_col),
        out_shape=(grad, grad, jax.ShapeDtypeStruct((1, 1), jnp.float32)),
        in_specs=[pl.BlockSpec(memory_space=pltpu.HBM)] * 2,
        out_specs=(space,) * 3,
        scratch_shapes=[
            pltpu.VMEM((2, n_dev, shard), jnp.bfloat16),
            pltpu.VMEM((n_chunks, 2, n_dev, width), jnp.bfloat16),
            pltpu.VMEM((2, 2, n_dev, shard), jnp.bfloat16),
            pltpu.VMEM((2, TILE, shard), jnp.float32),
            pltpu.VMEM((2, 2, shard), jnp.float32),
            pltpu.VMEM((2, n_dev, LANES), jnp.float32),
            pltpu.VMEM((2, n_dev, LANES), jnp.float32),
            pltpu.VMEM((1, width), jnp.float32),
            own_part,
            own_part,
            own_part,
            own_part,
            own_part,
            own_part,
            pltpu.VMEM((n_plane, TILE, LANES), jnp.float32),
            pltpu.VMEM((2, rows + TILE, LANES), jnp.float32),
            chunk_sems,
            chunk_sems,
            chunk_sems,
            pair_sems,
            pair_sems,
        ]
        + [plane_sems] * 10,
        compiler_params=pltpu.CompilerParams(
            collective_id=0, has_side_effects=True, vmem_limit_bytes=48 * 1024 * 1024
        ),
    )(view_a, view_b)
    return (grad_a, grad_b, loss.reshape(()))


def solution(mesh):
    in_specs = (P("dp", ("row", "col")), P("dp", ("row", "col")))
    out_specs = (P("dp", ("row", "col")), P("dp", ("row", "col")), P())
    return jax.shard_map(
        on_device, mesh=mesh, in_specs=in_specs, out_specs=out_specs, check_vma=False
    )
```

```python
import functools

import jax
import jax.numpy as jnp
from jax import lax
from jax.experimental import pallas as pl
from jax.experimental.pallas import tpu as pltpu
from jax.sharding import PartitionSpec as P

LANES = 128
TILE = 8
MESH = pl.DeviceIdType.MESH


def plain(view_a, view_b):
    n_dp = lax.axis_size("dp")
    n_parts = lax.axis_size("row") * lax.axis_size("col")
    dp_index = lax.axis_index("dp")
    n_dev, shard = view_a.shape
    total = n_dev * n_dp
    f_all = shard * n_parts
    coef = 2.0 * total / (25.0 * (total - 1))
    share = shard // n_dp

    own = jnp.stack([view_a, view_b])
    full = lax.all_gather(own, "dp", axis=1, tiled=True).astype(jnp.float32)
    mean = jnp.sum(full, axis=1, keepdims=True) / total
    diff = full - mean
    std = jnp.sqrt(jnp.sum(diff * diff, axis=1, keepdims=True) / (total - 1) + 0.0001)
    cent = diff.astype(jnp.bfloat16)
    cent32 = cent.astype(jnp.float32)
    diag = jnp.sum(cent32 * cent32, axis=1, keepdims=True) / (total - 1)

    piece = lax.dynamic_slice_in_dim(cent, dp_index * share, share, 2)
    gram = lax.dot_general(
        piece, piece, (((2,), (2,)), ((0,), (0,))), preferred_element_type=jnp.float32
    )
    own32 = own.astype(jnp.float32)
    gap = own32[0] - own32[1]
    local = 25.0 * jnp.sum(gap * gap) / (total * f_all)
    per_feature = 25.0 * jnp.maximum(1.0 - std, 0.0) - diag * diag
    local = local + jnp.sum(per_feature) / (f_all * n_dp)
    gram, local = lax.psum((gram, local), ("dp", "row", "col"))
    gram = gram / (total - 1)
    objective = (local + jnp.sum(gram * gram) / f_all) * total / (50.0 * f_all)

    lean = gram - jnp.mean(gram, axis=1, keepdims=True)
    lean = lax.dynamic_slice_in_dim(lean, dp_index * n_dev, n_dev, 1)
    pull = lax.dot_general(
        lean,
        cent32,
        (((2,), (1,)), ((0,), (0,))),
        preferred_element_type=jnp.float32,
        precision=lax.Precision.HIGHEST,
    )
    mine = lax.dynamic_slice_in_dim(cent32, dp_index * n_dev, n_dev, 1)
    pull = pull - diag * (mine - jnp.mean(cent32, axis=1, keepdims=True))
    hinge = jnp.where(std < 1.0, total * (own32 - mean) / (2.0 * std * (total - 1)), 0.0)
    rest = coef * pull - hinge
    return (gap + rest[0], rest[1] - gap, objective)


def gram_kernel(
    n_row,
    n_col,
    view_a,
    view_b,
    grad_a,
    grad_b,
    loss_out,
    mine,
    other,
    cent,
    stats,
    sums,
    gram_own,
    gram_cross,
    local,
    out_own,
    in_own,
    all_own,
    out_cross,
    in_cross,
    all_cross,
    all_tail,
    pair,
    load_sem,
    view_send,
    view_recv,
    sums_sem,
    pair_sem,
    own_send,
    own_recv,
    own_all_send,
    own_all_recv,
    cross_send,
    cross_recv,
    cross_all_send,
    cross_all_recv,
    tail_send,
    tail_recv,
):
    views = (view_a, view_b)
    grads = (grad_a, grad_b)
    n_dev, shard = view_a.shape
    total = 2 * n_dev
    n_plane = n_row * n_col
    f_all = shard * n_plane
    coef = 2.0 * total / (25.0 * (total - 1))
    n_chunks = other.shape[0]
    half = n_chunks // 2
    held = 2
    width = other.shape[3]
    rows = all_own.shape[1]
    dp = lax.axis_index("dp")
    me = lax.axis_index("row") * n_col + lax.axis_index("col")
    partner = {"dp": 1 - dp}

    def columns(c):
        return pl.ds(pl.multiple_of(c * width, width), width)

    def load(v, c):
        return pltpu.make_async_copy(
            views[v].at[:, columns(c)], mine.at[v, :, columns(c)], load_sem.at[c, v]
        )

    for c in range(n_chunks):
        load(0, c).start()
        load(1, c).start()

    def place(peer):
        return {"row": peer // n_col, "col": peer % n_col}

    barrier = pltpu.get_barrier_semaphore()
    pl.semaphore_signal(barrier, inc=1, device_id=partner, device_id_type=MESH)

    def greet(k, carry):
        peer = (me + k) % n_plane
        pl.semaphore_signal(barrier, inc=1, device_id=place(peer), device_id_type=MESH)
        return carry

    lax.fori_loop(1, n_plane, greet, 0)
    pl.semaphore_wait(barrier, n_plane)

    def to_partner(source, target, send_sem, recv_sem):
        return pltpu.make_async_remote_copy(
            src_ref=source,
            dst_ref=target,
            send_sem=send_sem,
            recv_sem=recv_sem,
            device_id=partner,
            device_id_type=MESH,
        )

    def view_copy(v, c):
        return to_partner(
            views[v].at[:, columns(c)], other.at[c, v], view_send.at[c, v], view_recv.at[c, v]
        )

    def send_views(k, carry):
        c = (half * (1 - dp) + k) % n_chunks
        view_copy(0, c).start()
        view_copy(1, c).start()
        return carry

    lax.fori_loop(0, 1, send_views, 0)

    def add_rows(x):
        return jnp.sum(x, axis=0, keepdims=True)

    def own_sums(c, carry):
        for v in range(2):
            load(v, c).wait()
            sums[0, v:v + 1, columns(c)] = add_rows(mine[v, :, columns(c)].astype(jnp.float32))
        return carry

    lax.fori_loop(0, n_chunks, own_sums, 0)
    sums_copy = to_partner(sums.at[0], sums.at[1], sums_sem.at[0], sums_sem.at[1])
    sums_copy.start()
    lax.fori_loop(1, 2, send_views, 0)
    gram_own[...] = jnp.zeros_like(gram_own)
    gram_cross[...] = jnp.zeros_like(gram_cross)
    local[...] = jnp.zeros_like(local)
    sums_copy.wait()
    dims = (((1,), (1,)), ((), ()))

    def center_own(c, carry):
        cols = columns(c)
        for v in range(2):
            mean = (sums[0, v:v + 1, cols] + sums[1, v:v + 1, cols]) / total
            diff = mine[v, :, cols].astype(jnp.float32) - mean
            kept = diff.astype(jnp.bfloat16)
            cent[v, dp, :, cols] = kept
            back = kept.astype(jnp.float32)
            stats[v, 0:1, cols] = mean
            stats[v, 4:5, cols] = add_rows(diff * diff)
            stats[v, 5:6, cols] = add_rows(back * back)
            stats[v, 6:7, cols] = add_rows(back)
            gram_own[v] += lax.dot_general(kept, kept, dims, preferred_element_type=jnp.float32)
        return carry

    lax.fori_loop(0, half, center_own, 0)
    lax.fori_loop(2, 3, send_views, 0)
    lax.fori_loop(half, n_chunks, center_own, 0)

    def exchange(source, target, send_sem, recv_sem, scatter):
        def copy(peer, slot):
            return pltpu.make_async_remote_copy(
                src_ref=source.at[peer if scatter else slot],
                dst_ref=target.at[slot],
                send_sem=send_sem.at[peer],
                recv_sem=recv_sem.at[slot],
                device_id=place(peer),
                device_id_type=MESH,
            )

        def start_one(k, carry):
            copy((me + k) % n_plane, me).start()
            return carry

        def end_one(k, carry):
            peer = (me + k) % n_plane
            copy(peer, me).wait_send()
            copy(peer, peer).wait_recv()
            return carry

        def start():
            lax.fori_loop(1, n_plane, start_one, 0)

        def end():
            lax.fori_loop(1, n_plane, end_one, 0)

        return start, end

    def added(ref):
        piece = ref[0]
        for r in range(1, n_plane):
            piece = piece + ref[r]
        return piece

    start_own, end_own = exchange(out_own, in_own, own_send, own_recv, True)
    start_own_all, end_own_all = exchange(all_own, all_own, own_all_send, own_all_recv, False)
    start_cross, end_cross = exchange(out_cross, in_cross, cross_send, cross_recv, True)
    start_cross_all, end_cross_all = exchange(
        all_cross, all_cross, cross_all_send, cross_all_recv, False
    )
    start_tail, end_tail = exchange(all_tail, all_tail, tail_send, tail_recv, False)
    per_block = n_dev // rows
    for r in range(n_plane):
        first = r % per_block * rows
        out_own[r] = gram_own[r // per_block, first:first + rows, :]
    start_own()
    in_own[me] = out_own[me]

    def take_chunk(k, multiply):
        c = (half * dp + k) % n_chunks
        cols = columns(c)
        both = [mine[v, :, cols].astype(jnp.float32) for v in range(2)]
        gap = both[0] - both[1]
        for v in range(2):
            view_copy(v, c).wait_recv()
            mean = stats[v, 0:1, cols]
            diff = other[c, v].astype(jnp.float32) - mean
            kept = diff.astype(jnp.bfloat16)
            cent[v, 1 - dp, :, cols] = kept
            back = kept.astype(jnp.float32)
            std = jnp.sqrt((stats[v, 4:5, cols] + add_rows(diff * diff)) / (total - 1) + 0.0001)
            diag = (stats[v, 5:6, cols] + add_rows(back * back)) / (total - 1)
            column = stats[v, 6:7, cols] + add_rows(back)
            slope = jnp.where(std < 1.0, total / (2.0 * std * (total - 1)), 0.0)
            own = cent[v, dp, :, cols].astype(jnp.float32)
            rest = slope * (both[v] - mean) + (coef * diag) * (own - column / total)
            grads[v][:, cols] = (gap if v == 0 else -gap) - rest
            if multiply:
                local[...] += (25.0 * jnp.maximum(1.0 - std, 0.0) - diag * diag) / f_all
                gram_cross[v] += lax.dot_general(
                    cent[v, 0, :, cols],
                    cent[v, 1, :, cols],
                    dims,
                    preferred_element_type=jnp.float32,
                )
        if multiply:
            gap_other = other[c, 0].astype(jnp.float32) - other[c, 1].astype(jnp.float32)
            squares = add_rows(gap * gap) + add_rows(gap_other * gap_other)
            local[...] += 25.0 * squares / (total * f_all)

    def take_chunks(first, last, multiply):
        def one(k, carry):
            take_chunk(k, multiply)
            return carry

        lax.fori_loop(first, last, one, 0)

    take_chunks(0, 1, True)
    lax.fori_loop(3, half, send_views, 0)
    end_own()
    all_own[me] = added(in_own)
    start_own_all()
    take_chunks(1, half - 1, True)
    lax.fori_loop(half, half + 1, send_views, 0)
    take_chunks(half - 1, half, True)
    lax.fori_loop(half + 1, n_chunks - held, send_views, 0)

    for r in range(n_plane):
        first = r % per_block * rows
        out_cross[r] = gram_cross[r // per_block, first:first + rows, :]
    start_cross()
    in_cross[me] = out_cross[me]
    end_own_all()

    def squared(ref):
        square = jnp.zeros((rows, LANES), jnp.float32)
        for r in range(n_plane):
            square = square + ref[r] * ref[r]
        return jnp.broadcast_to(jnp.sum(square).reshape(1, 1), (1, LANES))

    def whole(ref, v):
        return jnp.concatenate([ref[v * per_block + q] for q in range(per_block)], axis=0)

    pair[0, rows:rows + TILE, :] = jnp.concatenate(
        [
            add_rows(whole(all_own, 0)),
            add_rows(whole(all_own, 1)),
            jnp.broadcast_to(jnp.sum(local[...]).reshape(1, 1), (1, LANES)),
            squared(all_own),
            jnp.zeros((TILE - 4, LANES), jnp.float32),
        ],
        axis=0,
    )
    take_chunks(half, half + 1, False)
    end_cross()
    pair[0, 0:rows, :] = added(in_cross)
    pair_copy = to_partner(pair.at[0], pair.at[1], pair_sem.at[0], pair_sem.at[1])
    pair_copy.start()
    lax.fori_loop(n_chunks - held, n_chunks, send_views, 0)
    take_chunks(half + 1, n_chunks - held, False)
    pair_copy.wait()
    piece = pair[0] + pair[1]
    all_cross[me] = piece[0:rows, :]
    all_tail[me] = piece[rows:rows + TILE, :]
    start_cross_all()
    start_tail()
    take_chunks(n_chunks - held, n_chunks - 1, False)
    end_cross_all()

    first_half = jnp.full((n_dev, LANES), dp, jnp.int32) == 0
    factors = []
    for v in range(2):
        own = whole(all_own, v)
        cross = whole(all_cross, v)
        flipped = cross.T
        rest = jnp.where(first_half, flipped, cross)
        own = own - (add_rows(own) + add_rows(rest)) / total
        rest = jnp.where(first_half, cross, flipped)
        rest = rest - (add_rows(rest) + pair[1, rows + v:rows + v + 1, :]) / total
        left = jnp.where(first_half, own, rest)
        right = jnp.where(first_half, rest, own)
        factor = jnp.concatenate([left, right], axis=1) * (coef / (total - 1))
        one = factor.astype(jnp.bfloat16)
        rest = factor - one.astype(jnp.float32)
        two = rest.astype(jnp.bfloat16)
        three = (rest - two.astype(jnp.float32)).astype(jnp.bfloat16)
        factors.append(jnp.concatenate([one, two, three], axis=0))

    def give_chunk(k, carry):
        cols = columns((half * dp + k) % n_chunks)
        for v in range(2):
            right = cent[v, :, :, cols].reshape(total, width)
            pull = jnp.dot(factors[v], right, preferred_element_type=jnp.float32)
            grads[v][:, cols] += pull[0:n_dev] + pull[n_dev:total] + pull[total:total + n_dev]
        return carry

    lax.fori_loop(0, n_chunks - 1, give_chunk, 0)
    take_chunks(n_chunks - 1, n_chunks, False)
    lax.fori_loop(n_chunks - 1, n_chunks, give_chunk, 0)

    end_tail()
    square = all_tail[me][3:4, :] + 2.0 * squared(all_cross)
    loss = added(all_tail)[2:3, :] + square / (float(total - 1) * float(total - 1) * f_all)
    loss_out[...] = loss[0:1, 0:1] * (total / (50.0 * f_all))

    def end_views(c, carry):
        view_copy(0, c).wait_send()
        view_copy(1, c).wait_send()
        return carry

    lax.fori_loop(0, n_chunks, end_views, 0)


def on_device(view_a, view_b):
    n_row = lax.axis_size("row")
    n_col = lax.axis_size("col")
    n_plane = n_row * n_col
    n_dev, shard = view_a.shape
    total = 2 * n_dev
    rows = total // n_plane
    n_chunks = 8
    width = shard // n_chunks
    fits = n_dev == LANES and rows > 0 and rows % TILE == 0 and n_dev % rows == 0
    if lax.axis_size("dp") != 2 or not fits or shard % (n_chunks * LANES):
        return plain(view_a, view_b)
    space = pl.BlockSpec(memory_space=pltpu.VMEM)
    grad = jax.ShapeDtypeStruct((n_dev, shard), jnp.float32)
    view_a = pltpu.with_memory_space_constraint(view_a, pltpu.HBM)
    view_b = pltpu.with_memory_space_constraint(view_b, pltpu.HBM)
    own_part = pltpu.VMEM((n_plane, rows, LANES), jnp.float32)
    plane_sems = pltpu.SemaphoreType.DMA((n_plane,))
    chunk_sems = pltpu.SemaphoreType.DMA((n_chunks, 2))
    pair_sems = pltpu.SemaphoreType.DMA((2,))
    grad_a, grad_b, loss = pl.pallas_call(
        functools.partial(gram_kernel, n_row, n_col),
        out_shape=(grad, grad, jax.ShapeDtypeStruct((1, 1), jnp.float32)),
        in_specs=[pl.BlockSpec(memory_space=pltpu.HBM)] * 2,
        out_specs=(space,) * 3,
        scratch_shapes=[
            pltpu.VMEM((2, n_dev, shard), jnp.bfloat16),
            pltpu.VMEM((n_chunks, 2, n_dev, width), jnp.bfloat16),
            pltpu.VMEM((2, 2, n_dev, shard), jnp.bfloat16),
            pltpu.VMEM((2, TILE, shard), jnp.float32),
            pltpu.VMEM((2, 2, shard), jnp.float32),
            pltpu.VMEM((2, n_dev, LANES), jnp.float32),
            pltpu.VMEM((2, n_dev, LANES), jnp.float32),
            pltpu.VMEM((1, width), jnp.float32),
            own_part,
            own_part,
            own_part,
            own_part,
            own_part,
            own_part,
            pltpu.VMEM((n_plane, TILE, LANES), jnp.float32),
            pltpu.VMEM((2, rows + TILE, LANES), jnp.float32),
            chunk_sems,
            chunk_sems,
            chunk_sems,
            pair_sems,
            pair_sems,
        ]
        + [plane_sems] * 10,
        compiler_params=pltpu.CompilerParams(
            collective_id=0, has_side_effects=True, vmem_limit_bytes=48 * 1024 * 1024
        ),
    )(view_a, view_b)
    return (grad_a, grad_b, loss.reshape(()))


def solution(mesh):
    in_specs = (P("dp", ("row", "col")), P("dp", ("row", "col")))
    out_specs = (P("dp", ("row", "col")), P("dp", ("row", "col")), P())
    return jax.shard_map(
        on_device, mesh=mesh, in_specs=in_specs, out_specs=out_specs, check_vma=False
    )
```
